32 devices in a mesh: scene: 4 (over z), view: 8 (over y, x, core).
Axes of the slice: x: 2, y: 2, z: 4, core: 2. Of those that a mesh axis runs over, the one named last changes fastest.
Arguments:
- queries: bfloat16 [8192, 1024], P(('scene', 'view')), parts along dimension 0, may hold values from -256 to 256
- keys: bfloat16 [8192, 1024], P(('scene', 'view')), parts along dimension 0, may hold values from -6 to 6
- values: bfloat16 [8192, 1024], P(('scene', 'view')), parts along dimension 0, may hold values from -6 to 6
- grad_out: bfloat16 [8192, 1024], P(('scene', 'view')), parts along dimension 0, may hold values from -6 to 6
- pairs: int32 [64, 4], P(('scene', 'view')), parts along dimension 0, may hold values from 0 to 15, as said below
- counts: int32 [64], P(('scene', 'view')), parts along dimension 0, may hold values from 0 to 4, as said below
Outputs:
- attended: bfloat16 [8192, 1024], P(('scene', 'view')), parts along dimension 0
- grad_queries: bfloat16 [8192, 1024], P(('scene', 'view')), parts along dimension 0
- grad_keys: bfloat16 [8192, 1024], P(('scene', 'view')), parts along dimension 0
- grad_values: bfloat16 [8192, 1024], P(('scene', 'view')), parts along dimension 0
The draws below stay inside these ranges and needn't reach their ends.
There are 4 independent parts, one for each index of `scene`. The reference program is written for one: setup_inputs(seed, part) draws one part's arguments, and reference() takes and returns one part's arrays. A program takes and returns all parts, laid end to end along the dimension named above; each array names one. Nothing has to cross between parts.
Inputs may be any that keep to these rules, and one draw needn't show every extreme that they name: The first counts[v] entries of row v of pairs are distinct blocks at cycle distance 1 or 2 from v; the other entries are blocks of that kind too and are not used. `counts`: some block uses all 4 entries.
All inputs are finite; a program needn't handle non-finite values.
Results may differ from the reference program's by a relative error of at most 0.0078.
Values may be sent and summed in bfloat16 or wider, within the bound.
A program may use at most 64 MiB of HBM per device.

```python
import jax
import jax.numpy as jnp
from jax import lax

D = 1024
HEADS = 16
HEAD_DIM = 64
VIEW_TOK = 128
MAX_PAIRS = 4
VIEWS = 16
TOKENS = 2048


def pair_table(key):
    key = jax.random.fold_in(key, 101)
    first, second, third, fourth = jax.random.split(key, 4)
    heavy = jax.random.randint(first, (VIEWS,), 0, 4) == 0
    light = jax.random.randint(second, (VIEWS,), 0, 2)
    count_list = jnp.where(heavy, MAX_PAIRS, light)
    full_view = jax.random.randint(third, (), 0, VIEWS)
    count_list = jnp.where(jnp.arange(VIEWS) == full_view, MAX_PAIRS, count_list).astype(jnp.int32)
    ranks = jax.random.randint(fourth, (VIEWS, 4), 0, 1000) * 4 + jnp.arange(4)[None, :]
    order = jnp.argsort(ranks, axis=1)
    steps = jnp.array([-2, -1, 1, 2], jnp.int32)
    pair_list = (jnp.arange(VIEWS)[:, None] + jnp.take(steps, order) + VIEWS) % VIEWS
    return (pair_list.astype(jnp.int32), count_list)


def draw_pairs(key, part):
    shared = pair_table(key)
    return shared[0]


def draw_counts(key, part):
    shared = pair_table(key)
    return shared[1]


def key_rows(key):
    key = jax.random.fold_in(key, 202)
    return jnp.clip(jax.random.normal(key, (TOKENS, D), jnp.float32), -5.0, 5.0)


def draw_keys(key, part):
    base = key_rows(key)
    return base.astype(jnp.bfloat16)


def draw_queries(key, part):
    key = jax.random.fold_in(key, 4)
    first = jax.random.fold_in(key, 0)
    return jnp.clip(jax.random.normal(first, (TOKENS, D), jnp.float32), -5.0, 5.0).astype(jnp.bfloat16)


def shard_levels(stream_key, shape, pieces, least, largest):
    level, own = 1.0, jax.random.fold_in(stream_key, 6)
    for axis_at, shards_of in pieces:
        steps = jnp.exp(jax.random.uniform(jax.random.fold_in(own, axis_at), (shards_of,), jnp.float32, least / len(pieces), largest / len(pieces)))
        level = level * jnp.repeat(steps, shape[axis_at] // shards_of).reshape([-1 if axis == axis_at else 1 for axis in range(len(shape))])
    return level


def scatter_about(rng, extent, spread, limit, cuts=(), held_as=jnp.bfloat16):
    values = jax.random.normal(rng, extent, jnp.float32) * spread
    if len(cuts) > 0:
        values = shard_levels(rng, extent, cuts, -0.22, 0.18) * values
    return jnp.clip(values, min=-limit, max=limit).astype(held_as)


def setup_inputs(seed: int = 0, part: int = 0) -> dict:
    key_of = jax.random.split(jax.random.key(seed), 7)
    part_splits = jax.random.split(jax.random.fold_in(key_of[6], part), 7)
    return {
        "queries": draw_queries(jax.random.fold_in(jax.random.fold_in(key_of[6], part), 71), part),
        "keys": draw_keys(jax.random.fold_in(jax.random.fold_in(key_of[6], part), 71), part),
        "values": scatter_about(part_splits[2], (TOKENS, D), 1.0, 6.0, ((0, 8),)),
        "grad_out": scatter_about(part_splits[3], (TOKENS, D), 1.0, 6.0, ((0, 8),)),
        "pairs": draw_pairs(jax.random.fold_in(jax.random.fold_in(key_of[6], part), 71), part),
        "counts": draw_counts(jax.random.fold_in(jax.random.fold_in(key_of[6], part), 71), part),
    }


def heads(rows):
    return rows.reshape(rows.shape[0], HEADS, HEAD_DIM).astype(jnp.float32)


def reference(queries, keys, values, grad_out, pairs, counts):
    views = pairs.shape[0]
    offsets = jnp.arange(-2, 3, dtype=jnp.int32)
    scale = HEAD_DIM ** -0.5
    key_views = keys.reshape(views, VIEW_TOK, D)
    value_views = values.reshape(views, VIEW_TOK, D)

    def step(carry, view):
        key_acc, value_acc = carry
        window = ((view + offsets) % views).astype(jnp.int32)
        relative = (pairs[view] - view + views // 2) % views - views // 2
        live_slots = jnp.arange(MAX_PAIRS, dtype=jnp.int32) < counts[view]
        allowed = jnp.any((relative[:, None] == offsets[None, :]) & live_slots[:, None], axis=0) | (offsets == 0)
        live = jnp.repeat(allowed, VIEW_TOK)[None, None, :]
        k_rows = jnp.take(key_views, window, axis=0).reshape(5 * VIEW_TOK, D)
        v_rows = jnp.take(value_views, window, axis=0).reshape(5 * VIEW_TOK, D)
        q_rows = lax.dynamic_slice_in_dim(queries, view * VIEW_TOK, VIEW_TOK, 0)
        d_rows = lax.dynamic_slice_in_dim(grad_out, view * VIEW_TOK, VIEW_TOK, 0)
        scores = jnp.einsum("qhd,khd->hqk", heads(q_rows), heads(k_rows)) * scale
        kept = jnp.where(live, scores, -1e30)
        top = jnp.max(kept, axis=2)
        log_total = top + jnp.log(jnp.sum(jnp.exp(kept - top[:, :, None]), axis=2))
        weights = jnp.exp(kept - log_total[:, :, None])
        weights_b = lax.optimization_barrier(weights.astype(jnp.bfloat16)).astype(jnp.float32)
        out = jnp.einsum("hqk,khd->qhd", weights_b, heads(v_rows)).reshape(VIEW_TOK, D)
        delta = jnp.sum(heads(d_rows) * out.reshape(VIEW_TOK, HEADS, HEAD_DIM), axis=2).T
        prob_grad = jnp.einsum("qhd,khd->hqk", heads(d_rows), heads(v_rows))
        score_grad = (weights * (prob_grad - delta[:, :, None])).astype(jnp.bfloat16)
        score_grad = lax.optimization_barrier(score_grad).astype(jnp.float32)
        query_grads = jnp.einsum("hqk,khd->qhd", score_grad, heads(k_rows)).reshape(VIEW_TOK, D) * scale
        key_part = jnp.einsum("hqk,qhd->khd", score_grad, heads(q_rows)).reshape(5, VIEW_TOK, D) * scale
        value_part = jnp.einsum("hqk,qhd->khd", weights_b, heads(d_rows)).reshape(5, VIEW_TOK, D)
        key_acc = key_acc.at[window].add(key_part)
        value_acc = value_acc.at[window].add(value_part)
        return (key_acc, value_acc), (out.astype(jnp.bfloat16), query_grads.astype(jnp.bfloat16))

    start = (jnp.zeros((views, VIEW_TOK, D), jnp.float32), jnp.zeros((views, VIEW_TOK, D), jnp.float32))
    (key_acc, value_acc), (outs, query_grads) = lax.scan(step, start, jnp.arange(views, dtype=jnp.int32))
    attended = outs.reshape(views * VIEW_TOK, D)
    grad_queries = query_grads.reshape(views * VIEW_TOK, D)
    grad_keys = key_acc.reshape(views * VIEW_TOK, D).astype(jnp.bfloat16)
    grad_values = value_acc.reshape(views * VIEW_TOK, D).astype(jnp.bfloat16)
    return (attended, grad_queries, grad_keys, grad_values)
```

```python
import jax
import jax.numpy as jnp
from jax import lax
from jax.experimental import pallas as pl
from jax.experimental.pallas import tpu as pltpu
from jax.sharding import PartitionSpec as P

HEAD_DIM = 64
VIEW_TOK = 128
LANES = 2 * HEAD_DIM
MASKED = -1e30
REACH = 2


def nt(a, b):
    return lax.dot_general(a, b, (((1,), (1,)), ((), ())), preferred_element_type=jnp.float32)


def tn(a, b):
    return lax.dot_general(a, b, (((0,), (0,)), ((), ())), preferred_element_type=jnp.float32)


def nn(a, b):
    return jnp.dot(a, b, preferred_element_type=jnp.float32)


def two_heads(rows):
    first = lax.broadcasted_iota(jnp.int32, rows.shape, 1) < HEAD_DIM
    zero = jnp.zeros_like(rows)
    return jnp.concatenate([jnp.where(first, rows, zero), jnp.where(first, zero, rows)], axis=0)


def fold_heads(wide):
    first = lax.broadcasted_iota(jnp.int32, (LANES, VIEW_TOK), 0) < HEAD_DIM
    return jnp.where(first, wide[:, :VIEW_TOK], wide[:, VIEW_TOK:])


def block_bias(pairs, counts, view, own, views, offset):
    target = lax.rem(own + offset + views, views)
    live = jnp.bool_(False)
    for slot in range(pairs.shape[1]):
        live = live | ((pairs[view, slot] == target) & (slot < counts[view]))
    return jnp.where(live, 0.0, MASKED).astype(jnp.float32)


def attend(q, d, k_win, v_win, biases):
    qs = two_heads((q.astype(jnp.float32) * HEAD_DIM ** -0.5).astype(jnp.bfloat16))
    ds = two_heads(d)
    scores = nt(k_win, qs)
    tiles = []
    for j, bias in enumerate(biases):
        tile = scores[j * VIEW_TOK : (j + 1) * VIEW_TOK]
        tiles.append(tile if bias is None else tile + bias)
    scores = jnp.concatenate(tiles, axis=0)
    grown = jnp.exp(scores - jnp.max(scores, axis=0, keepdims=True))
    weights = grown * (1.0 / jnp.sum(grown, axis=0, keepdims=True))
    weights_b = weights.astype(jnp.bfloat16)
    out = fold_heads(tn(v_win, weights_b))
    product = out * d.astype(jnp.float32).T
    delta = jnp.concatenate(
        [
            jnp.sum(product[:HEAD_DIM], axis=0, keepdims=True),
            jnp.sum(product[HEAD_DIM:], axis=0, keepdims=True),
        ],
        axis=1,
    )
    score_grad = (weights * (nt(v_win, ds) - delta)).astype(jnp.bfloat16)
    grad_q = fold_heads(tn(k_win, score_grad)) * HEAD_DIM ** -0.5
    return (
        out.T.astype(jnp.bfloat16),
        grad_q.T.astype(jnp.bfloat16),
        nn(score_grad, qs),
        nn(weights_b, ds),
    )


def kernel(
    size, chunks,
    pairs, counts, q_ref, k_ref, v_ref, d_ref,
    a_ref, gq_ref, gk_ref, gv_ref,
    k_in, v_in, g_out, g_in, own_k, own_v,
    kv_send, kv_recv, g_send, g_recv,
):
    me = lax.axis_index("view")
    peers = (lax.rem(me + size - 1, size), lax.rem(me + 1, size))
    span = q_ref.shape[0]
    local_views = span // VIEW_TOK
    views = size * local_views

    barrier = pltpu.get_barrier_semaphore()
    for peer in peers:
        pl.semaphore_signal(
            barrier, inc=1, device_id={"view": peer}, device_id_type=pl.DeviceIdType.MESH
        )
    pl.semaphore_wait(barrier, 2)

    def columns(c):
        return pl.ds(pl.multiple_of(c * LANES, LANES), LANES)

    def kv_copy(c, side, which):
        src, dst = ((k_ref, k_in), (v_ref, v_in))[which]
        return pltpu.make_async_remote_copy(
            src_ref=src.at[:, columns(c)],
            dst_ref=dst.at[1 - side, c],
            send_sem=kv_send.at[side, which, c],
            recv_sem=kv_recv.at[1 - side, which, c],
            device_id={"view": peers[side]},
            device_id_type=pl.DeviceIdType.MESH,
        )

    def grad_copy(c, side):
        return pltpu.make_async_remote_copy(
            src_ref=g_out.at[side, c],
            dst_ref=g_in.at[1 - side, c],
            send_sem=g_send.at[side, c],
            recv_sem=g_recv.at[1 - side, c],
            device_id={"view": peers[side]},
            device_id_type=pl.DeviceIdType.MESH,
        )

    def send_all(c, _):
        for which in (0, 1):
            for side in (0, 1):
                kv_copy(c, side, which).start()
        return 0

    lax.fori_loop(0, chunks, send_all, 0)

    biases = []
    for view in range(local_views):
        own = me * local_views + view
        biases.append(
            [
                None if offset == 0 else block_bias(pairs, counts, view, own, views, offset)
                for offset in range(-REACH, REACH + 1)
            ]
        )

    def work(c, _):
        for which in (0, 1):
            for side in (0, 1):
                kv_copy(c, side, which).wait_recv()
        cols = columns(c)
        k_all = jnp.concatenate([k_in[0, c], k_ref[:, cols], k_in[1, c]], axis=0)
        v_all = jnp.concatenate([v_in[0, c], v_ref[:, cols], v_in[1, c]], axis=0)
        sums = [[None] * (3 * local_views), [None] * (3 * local_views)]
        for view in range(local_views):
            rows = slice(view * VIEW_TOK, (view + 1) * VIEW_TOK)
            base = local_views + view - REACH
            win = slice(base * VIEW_TOK, (base + 2 * REACH + 1) * VIEW_TOK)
            out, grad_q, part_k, part_v = attend(
                q_ref[rows, cols], d_ref[rows, cols], k_all[win], v_all[win], biases[view]
            )
            a_ref[rows, cols] = out
            gq_ref[rows, cols] = grad_q
            for total, part in zip(sums, (part_k, part_v)):
                for j in range(2 * REACH + 1):
                    tile = part[j * VIEW_TOK : (j + 1) * VIEW_TOK]
                    at = base + j
                    total[at] = tile if total[at] is None else total[at] + tile
        for which, (total, kept) in enumerate(zip(sums, (own_k, own_v))):
            for j in range(local_views):
                rows = slice(j * VIEW_TOK, (j + 1) * VIEW_TOK)
                g_out[0, c, which, rows] = total[j].astype(jnp.bfloat16)
                g_out[1, c, which, rows] = total[2 * local_views + j].astype(jnp.bfloat16)
                kept[c, rows] = total[local_views + j]
        for side in (0, 1):
            grad_copy(c, side).start()
        return 0

    lax.fori_loop(0, chunks, work, 0)

    def finish(c, _):
        cols = columns(c)
        for side in (0, 1):
            grad_copy(c, side).wait_recv()
        for which, (kept, result) in enumerate(((own_k, gk_ref), (own_v, gv_ref))):
            total = (
                kept[c]
                + g_in[0, c, which].astype(jnp.float32)
                + g_in[1, c, which].astype(jnp.float32)
            )
            result[:, cols] = total.astype(jnp.bfloat16)
        return 0

    lax.fori_loop(0, chunks, finish, 0)

    def drain(c, _):
        for side in (0, 1):
            for which in (0, 1):
                kv_copy(c, side, which).wait_send()
            grad_copy(c, side).wait_send()
        return 0

    lax.fori_loop(0, chunks, drain, 0)


def body(queries, keys, values, grad_out, pairs, counts):
    size = lax.axis_size("view")
    span, width = queries.shape
    chunks = width // LANES
    assert span == REACH * VIEW_TOK
    vmem = pl.BlockSpec(memory_space=pltpu.VMEM)
    smem = pl.BlockSpec(memory_space=pltpu.SMEM)

    def run(*refs):
        kernel(size, chunks, *refs)

    pair_flops = 2 * 6 * 2 * 2 * VIEW_TOK * 5 * VIEW_TOK * LANES
    return pl.pallas_call(
        run,
        name="windowed_attention",
        out_shape=[jax.ShapeDtypeStruct((span, width), jnp.bfloat16)] * 4,
        in_specs=[smem, smem] + [vmem] * 4,
        out_specs=[vmem] * 4,
        scratch_shapes=[
            pltpu.VMEM((2, chunks, span, LANES), jnp.bfloat16),
            pltpu.VMEM((2, chunks, span, LANES), jnp.bfloat16),
            pltpu.VMEM((2, chunks, 2, span, LANES), jnp.bfloat16),
            pltpu.VMEM((2, chunks, 2, span, LANES), jnp.bfloat16),
            pltpu.VMEM((chunks, span, LANES), jnp.float32),
            pltpu.VMEM((chunks, span, LANES), jnp.float32),
            pltpu.SemaphoreType.DMA((2, 2, chunks)),
            pltpu.SemaphoreType.DMA((2, 2, chunks)),
            pltpu.SemaphoreType.DMA((2, chunks)),
            pltpu.SemaphoreType.DMA((2, chunks)),
        ],
        cost_estimate=pl.CostEstimate(
            flops=chunks * pair_flops,
            bytes_accessed=8 * span * width * 2,
            transcendentals=chunks * 4 * VIEW_TOK * 5 * VIEW_TOK,
        ),
        compiler_params=pltpu.CompilerParams(
            collective_id=0, has_side_effects=True, vmem_limit_bytes=40 * 1024 * 1024
        ),
    )(pairs, counts, queries, keys, values, grad_out)


def solution(mesh):
    rows = P(("scene", "view"), None)
    return jax.shard_map(
        body,
        mesh=mesh,
        in_specs=(rows, rows, rows, rows, rows, P(("scene", "view"))),
        out_specs=(rows, rows, rows, rows),
        check_vma=False,
    )
```

```python
import jax
import jax.numpy as jnp
from jax import lax
from jax.experimental import pallas as pl
from jax.experimental.pallas import tpu as pltpu
from jax.sharding import PartitionSpec as P

HEAD_DIM = 64
VIEW_TOK = 128
LANES = 2 * HEAD_DIM
MASKED = -1e30
REACH = 2
VMEM_BYTES = 60 * 1024 * 1024


def nt(a, b):
    return lax.dot_general(a, b, (((1,), (1,)), ((), ())), preferred_element_type=jnp.float32)


def tn(a, b):
    return lax.dot_general(a, b, (((0,), (0,)), ((), ())), preferred_element_type=jnp.float32)


def nn(a, b):
    return jnp.dot(a, b, preferred_element_type=jnp.float32)


def two_heads(rows):
    first = lax.broadcasted_iota(jnp.int32, rows.shape, 1) < HEAD_DIM
    zero = jnp.zeros_like(rows)
    return jnp.concatenate([jnp.where(first, rows, zero), jnp.where(first, zero, rows)], axis=0)


def fold_heads(wide):
    first = lax.broadcasted_iota(jnp.int32, (LANES, VIEW_TOK), 0) < HEAD_DIM
    return jnp.where(first, wide[:, :VIEW_TOK], wide[:, VIEW_TOK:])


def block_bias(pairs, counts, view, own, views, offset):
    target = lax.rem(own + offset + views, views)
    live = jnp.bool_(False)
    for slot in range(pairs.shape[1]):
        live = live | ((pairs[view, slot] == target) & (slot < counts[view]))
    return jnp.where(live, 0.0, MASKED).astype(jnp.float32)


def attend(q, d, k_win, v_win, biases):
    qs = two_heads((q.astype(jnp.float32) * HEAD_DIM ** -0.5).astype(jnp.bfloat16))
    ds = two_heads(d)
    scores = nt(k_win, qs)
    tiles = []
    for j, bias in enumerate(biases):
        tile = scores[j * VIEW_TOK : (j + 1) * VIEW_TOK]
        tiles.append(tile if bias is None else tile + bias)
    scores = jnp.concatenate(tiles, axis=0)
    grown = jnp.exp(scores - jnp.max(scores, axis=0, keepdims=True))
    weights = grown * (1.0 / jnp.sum(grown, axis=0, keepdims=True))
    weights_b = weights.astype(jnp.bfloat16)
    out = fold_heads(tn(v_win, weights_b))
    product = out * d.astype(jnp.float32).T
    delta = jnp.concatenate(
        [
            jnp.sum(product[:HEAD_DIM], axis=0, keepdims=True),
            jnp.sum(product[HEAD_DIM:], axis=0, keepdims=True),
        ],
        axis=1,
    )
    score_grad = (weights * (nt(v_win, ds) - delta)).astype(jnp.bfloat16)
    grad_q = fold_heads(tn(k_win, score_grad)) * HEAD_DIM ** -0.5
    return (
        out.T.astype(jnp.bfloat16),
        grad_q.T.astype(jnp.bfloat16),
        nn(score_grad, qs),
        nn(weights_b, ds),
    )


def kernel(
    size, chunks,
    pairs_hbm, counts_hbm, q_hbm, k_hbm, v_hbm, d_hbm,
    a_hbm, gq_hbm, gk_hbm, gv_hbm,
    pairs, counts, q_ref, k_ref, v_ref, d_ref, fetched,
    a_ref, gq_ref, gk_ref, gv_ref, stored, stored_part,
    k_in, v_in, g_out, g_in, own_k, own_v,
    kv_send, kv_recv, g_send, g_recv,
):
    me = lax.axis_index("view")
    peers = (lax.rem(me + size - 1, size), lax.rem(me + 1, size))
    span = q_ref.shape[0]
    local_views = span // VIEW_TOK
    views = size * local_views

    fetches = [
        pltpu.make_async_copy(src, dst, fetched.at[i])
        for i, (src, dst) in enumerate(
            (
                (k_hbm, k_ref),
                (v_hbm, v_ref),
                (q_hbm, q_ref),
                (d_hbm, d_ref),
                (pairs_hbm, pairs),
                (counts_hbm, counts),
            )
        )
    ]
    for fetch in fetches:
        fetch.start()

    barrier = pltpu.get_barrier_semaphore()
    for peer in peers:
        pl.semaphore_signal(
            barrier, inc=1, device_id={"view": peer}, device_id_type=pl.DeviceIdType.MESH
        )
    for fetch in fetches[:2]:
        fetch.wait()
    pl.semaphore_wait(barrier, 2)

    def columns(c):
        return pl.ds(pl.multiple_of(c * LANES, LANES), LANES)

    def kv_copy(c, side, which):
        src, dst = ((k_ref, k_in), (v_ref, v_in))[which]
        return pltpu.make_async_remote_copy(
            src_ref=src.at[:, columns(c)],
            dst_ref=dst.at[1 - side, c],
            send_sem=kv_send.at[side, which, c],
            recv_sem=kv_recv.at[1 - side, which, c],
            device_id={"view": peers[side]},
            device_id_type=pl.DeviceIdType.MESH,
        )

    def grad_copy(c, side):
        return pltpu.make_async_remote_copy(
            src_ref=g_out.at[side, c],
            dst_ref=g_in.at[1 - side, c],
            send_sem=g_send.at[side, c],
            recv_sem=g_recv.at[1 - side, c],
            device_id={"view": peers[side]},
            device_id_type=pl.DeviceIdType.MESH,
        )

    def send_all(c, _):
        for which in (0, 1):
            for side in (0, 1):
                kv_copy(c, side, which).start()
        return 0

    lax.fori_loop(0, chunks, send_all, 0)

    for fetch in fetches[2:]:
        fetch.wait()
    biases = []
    for view in range(local_views):
        own = me * local_views + view
        biases.append(
            [
                None if offset == 0 else block_bias(pairs, counts, view, own, views, offset)
                for offset in range(-REACH, REACH + 1)
            ]
        )

    def work(c, _):
        for which in (0, 1):
            for side in (0, 1):
                kv_copy(c, side, which).wait_recv()
        cols = columns(c)
        k_all = jnp.concatenate([k_in[0, c], k_ref[:, cols], k_in[1, c]], axis=0)
        v_all = jnp.concatenate([v_in[0, c], v_ref[:, cols], v_in[1, c]], axis=0)
        sums = [[None] * (3 * local_views), [None] * (3 * local_views)]
        for view in range(local_views):
            rows = slice(view * VIEW_TOK, (view + 1) * VIEW_TOK)
            base = local_views + view - REACH
            win = slice(base * VIEW_TOK, (base + 2 * REACH + 1) * VIEW_TOK)
            out, grad_q, part_k, part_v = attend(
                q_ref[rows, cols], d_ref[rows, cols], k_all[win], v_all[win], biases[view]
            )
            a_ref[rows, cols] = out
            gq_ref[rows, cols] = grad_q
            for total, part in zip(sums, (part_k, part_v)):
                for j in range(2 * REACH + 1):
                    tile = part[j * VIEW_TOK : (j + 1) * VIEW_TOK]
                    at = base + j
                    total[at] = tile if total[at] is None else total[at] + tile
        for which, (total, kept) in enumerate(zip(sums, (own_k, own_v))):
            for j in range(local_views):
                rows = slice(j * VIEW_TOK, (j + 1) * VIEW_TOK)
                g_out[0, c, which, rows] = total[j].astype(jnp.bfloat16)
                g_out[1, c, which, rows] = total[2 * local_views + j].astype(jnp.bfloat16)
                kept[c, rows] = total[local_views + j]
        for side in (0, 1):
            grad_copy(c, side).start()
        return 0

    lax.fori_loop(0, chunks, work, 0)

    stores = [
        pltpu.make_async_copy(a_ref, a_hbm, stored.at[0]),
        pltpu.make_async_copy(gq_ref, gq_hbm, stored.at[1]),
    ]
    for copy in stores:
        copy.start()

    def part_store(c, which):
        src, dst = ((gk_ref, gk_hbm), (gv_ref, gv_hbm))[which]
        cols = columns(c)
        return pltpu.make_async_copy(
            src.at[:, cols], dst.at[:, cols], stored_part.at[which, c]
        )

    def finish(c, _):
        cols = columns(c)
        for side in (0, 1):
            grad_copy(c, side).wait_recv()
        for which, (kept, result) in enumerate(((own_k, gk_ref), (own_v, gv_ref))):
            total = (
                kept[c]
                + g_in[0, c, which].astype(jnp.float32)
                + g_in[1, c, which].astype(jnp.float32)
            )
            result[:, cols] = total.astype(jnp.bfloat16)
            part_store(c, which).start()
        return 0

    lax.fori_loop(0, chunks, finish, 0)

    def drain(c, _):
        for side in (0, 1):
            for which in (0, 1):
                kv_copy(c, side, which).wait_send()
            grad_copy(c, side).wait_send()
        for which in (0, 1):
            part_store(c, which).wait()
        return 0

    lax.fori_loop(0, chunks, drain, 0)
    for copy in stores:
        copy.wait()


def store(*refs):
    count = (len(refs) - 1) // 2
    stored = refs[-1]
    copies = [
        pltpu.make_async_copy(refs[i], refs[count + i], stored.at[i]) for i in range(count)
    ]
    for copy in copies:
        copy.start()
    for copy in copies:
        copy.wait()


def body(queries, keys, values, grad_out, pairs, counts):
    size = lax.axis_size("view")
    span, width = queries.shape
    chunks = width // LANES
    assert span == REACH * VIEW_TOK
    hbm = pl.BlockSpec(memory_space=pltpu.HBM)

    def run(*refs):
        kernel(size, chunks, *refs)

    pair_flops = 2 * 6 * 2 * 2 * VIEW_TOK * 5 * VIEW_TOK * LANES
    block = jax.ShapeDtypeStruct((span, width), jnp.bfloat16)
    results = pl.pallas_call(
        run,
        name="windowed_attention",
        out_shape=[block] * 4,
        in_specs=[hbm] * 6,
        out_specs=[hbm] * 4,
        scratch_shapes=[
            pltpu.SMEM(pairs.shape, pairs.dtype),
            pltpu.SMEM(counts.shape, counts.dtype),
            pltpu.VMEM((span, width), jnp.bfloat16),
            pltpu.VMEM((span, width), jnp.bfloat16),
            pltpu.VMEM((span, width), jnp.bfloat16),
            pltpu.VMEM((span, width), jnp.bfloat16),
            pltpu.SemaphoreType.DMA((6,)),
            pltpu.VMEM((span, width), jnp.bfloat16),
            pltpu.VMEM((span, width), jnp.bfloat16),
            pltpu.VMEM((span, width), jnp.bfloat16),
            pltpu.VMEM((span, width), jnp.bfloat16),
            pltpu.SemaphoreType.DMA((2,)),
            pltpu.SemaphoreType.DMA((2, chunks)),
            pltpu.VMEM((2, chunks, span, LANES), jnp.bfloat16),
            pltpu.VMEM((2, chunks, span, LANES), jnp.bfloat16),
            pltpu.VMEM((2, chunks, 2, span, LANES), jnp.bfloat16),
            pltpu.VMEM((2, chunks, 2, span, LANES), jnp.bfloat16),
            pltpu.VMEM((chunks, span, LANES), jnp.float32),
            pltpu.VMEM((chunks, span, LANES), jnp.float32),
            pltpu.SemaphoreType.DMA((2, 2, chunks)),
            pltpu.SemaphoreType.DMA((2, 2, chunks)),
            pltpu.SemaphoreType.DMA((2, chunks)),
            pltpu.SemaphoreType.DMA((2, chunks)),
        ],
        cost_estimate=pl.CostEstimate(
            flops=chunks * pair_flops,
            bytes_accessed=8 * span * width * 2,
            transcendentals=chunks * 4 * VIEW_TOK * 5 * VIEW_TOK,
        ),
        compiler_params=pltpu.CompilerParams(
            collective_id=0, has_side_effects=True, vmem_limit_bytes=VMEM_BYTES
        ),
    )(pairs, counts, queries, keys, values, grad_out)
    return pl.pallas_call(
        store,
        name="store_results",
        out_shape=[block] * 4,
        in_specs=[hbm] * 4,
        out_specs=[hbm] * 4,
        scratch_shapes=[pltpu.SemaphoreType.DMA((4,))],
        compiler_params=pltpu.CompilerParams(vmem_limit_bytes=VMEM_BYTES),
    )(*results)


def solution(mesh):
    rows = P(("scene", "view"), None)
    return jax.shard_map(
        body,
        mesh=mesh,
        in_specs=(rows, rows, rows, rows, rows, P(("scene", "view"))),
        out_specs=(rows, rows, rows, rows),
        check_vma=False,
    )
```

```python
import functools

import jax
import jax.numpy as jnp
from jax import lax
from jax.experimental import pallas as pl
from jax.experimental.pallas import tpu as pltpu
from jax.sharding import PartitionSpec as P

HEAD_DIM = 64
VIEW_TOK = 128
LANES = 2 * HEAD_DIM
MASKED = -1e30
REACH = 2
VMEM_BYTES = 60 * 1024 * 1024


def nt(a, b):
    return lax.dot_general(a, b, (((1,), (1,)), ((), ())), preferred_element_type=jnp.float32)


def tn(a, b):
    return lax.dot_general(a, b, (((0,), (0,)), ((), ())), preferred_element_type=jnp.float32)


def nn(a, b):
    return jnp.dot(a, b, preferred_element_type=jnp.float32)


def two_heads(rows):
    first = lax.broadcasted_iota(jnp.int32, rows.shape, 1) < HEAD_DIM
    zero = jnp.zeros_like(rows)
    return jnp.concatenate([jnp.where(first, rows, zero), jnp.where(first, zero, rows)], axis=0)


def fold_heads(wide):
    first = lax.broadcasted_iota(jnp.int32, (LANES, VIEW_TOK), 0) < HEAD_DIM
    return jnp.where(first, wide[:, :VIEW_TOK], wide[:, VIEW_TOK:])


def block_bias(pairs, counts, view, own, views, offset):
    target = lax.rem(own + offset + views, views)
    live = jnp.bool_(False)
    for slot in range(pairs.shape[1]):
        live = live | ((pairs[view, slot] == target) & (slot < counts[view]))
    return jnp.where(live, 0.0, MASKED).astype(jnp.float32)


def attend(q, d, k_win, v_win, biases):
    qs = two_heads((q.astype(jnp.float32) * HEAD_DIM ** -0.5).astype(jnp.bfloat16))
    ds = two_heads(d)
    scores = nt(k_win, qs)
    tiles = []
    for j, bias in enumerate(biases):
        tile = scores[j * VIEW_TOK : (j + 1) * VIEW_TOK]
        tiles.append(tile if bias is None else tile + bias)
    scores = jnp.concatenate(tiles, axis=0)
    grown = jnp.exp(scores - jnp.max(scores, axis=0, keepdims=True))
    weights = grown * (1.0 / jnp.sum(grown, axis=0, keepdims=True))
    weights_b = weights.astype(jnp.bfloat16)
    out = fold_heads(tn(v_win, weights_b))
    product = out * d.astype(jnp.float32).T
    delta = jnp.concatenate(
        [
            jnp.sum(product[:HEAD_DIM], axis=0, keepdims=True),
            jnp.sum(product[HEAD_DIM:], axis=0, keepdims=True),
        ],
        axis=1,
    )
    score_grad = (weights * (nt(v_win, ds) - delta)).astype(jnp.bfloat16)
    grad_q = fold_heads(tn(k_win, score_grad)) * HEAD_DIM ** -0.5
    return (
        out.T.astype(jnp.bfloat16),
        grad_q.T.astype(jnp.bfloat16),
        nn(score_grad, qs),
        nn(weights_b, ds),
    )


def kernel(
    size, chunks,
    pairs_hbm, counts_hbm, q_hbm, k_hbm, v_hbm, d_hbm,
    a_hbm, gq_hbm, gk_hbm, gv_hbm,
    pairs, counts, q_ref, k_ref, v_ref, d_ref, fetched,
    a_ref, gq_ref, gk_ref, gv_ref, stored, stored_part,
    k_in, v_in, g_out, g_in, own_k, own_v,
    kv_send, kv_recv, g_send, g_recv,
):
    me = lax.axis_index("view")
    peers = (lax.rem(me + size - 1, size), lax.rem(me + 1, size))
    span = q_ref.shape[0]
    local_views = span // VIEW_TOK
    views = size * local_views

    fetches = [
        pltpu.make_async_copy(src, dst, fetched.at[i])
        for i, (src, dst) in enumerate(
            (
                (k_hbm, k_ref),
                (v_hbm, v_ref),
                (q_hbm, q_ref),
                (d_hbm, d_ref),
                (pairs_hbm, pairs),
                (counts_hbm, counts),
            )
        )
    ]
    for fetch in fetches:
        fetch.start()

    barrier = pltpu.get_barrier_semaphore()
    for peer in peers:
        pl.semaphore_signal(
            barrier, inc=1, device_id={"view": peer}, device_id_type=pl.DeviceIdType.MESH
        )
    for fetch in fetches[:2]:
        fetch.wait()
    pl.semaphore_wait(barrier, 2)

    def columns(c):
        return pl.ds(pl.multiple_of(c * LANES, LANES), LANES)

    def kv_copy(c, side, which):
        src, dst = ((k_ref, k_in), (v_ref, v_in))[which]
        return pltpu.make_async_remote_copy(
            src_ref=src.at[:, columns(c)],
            dst_ref=dst.at[1 - side, c],
            send_sem=kv_send.at[side, which, c],
            recv_sem=kv_recv.at[1 - side, which, c],
            device_id={"view": peers[side]},
            device_id_type=pl.DeviceIdType.MESH,
        )

    def grad_copy(c, side):
        return pltpu.make_async_remote_copy(
            src_ref=g_out.at[side, c],
            dst_ref=g_in.at[1 - side, c],
            send_sem=g_send.at[side, c],
            recv_sem=g_recv.at[1 - side, c],
            device_id={"view": peers[side]},
            device_id_type=pl.DeviceIdType.MESH,
        )

    def send_all(c, _):
        for which in (0, 1):
            for side in (0, 1):
                kv_copy(c, side, which).start()
        return 0

    lax.fori_loop(0, chunks, send_all, 0)

    for fetch in fetches[2:]:
        fetch.wait()
    biases = []
    for view in range(local_views):
        own = me * local_views + view
        biases.append(
            [
                None if offset == 0 else block_bias(pairs, counts, view, own, views, offset)
                for offset in range(-REACH, REACH + 1)
            ]
        )

    def work(c, _):
        for which in (0, 1):
            for side in (0, 1):
                kv_copy(c, side, which).wait_recv()
        cols = columns(c)
        k_all = jnp.concatenate([k_in[0, c], k_ref[:, cols], k_in[1, c]], axis=0)
        v_all = jnp.concatenate([v_in[0, c], v_ref[:, cols], v_in[1, c]], axis=0)
        sums = [[None] * (3 * local_views), [None] * (3 * local_views)]
        for view in range(local_views):
            rows = slice(view * VIEW_TOK, (view + 1) * VIEW_TOK)
            base = local_views + view - REACH
            win = slice(base * VIEW_TOK, (base + 2 * REACH + 1) * VIEW_TOK)
            out, grad_q, part_k, part_v = attend(
                q_ref[rows, cols], d_ref[rows, cols], k_all[win], v_all[win], biases[view]
            )
            a_ref[rows, cols] = out
            gq_ref[rows, cols] = grad_q
            for total, part in zip(sums, (part_k, part_v)):
                for j in range(2 * REACH + 1):
                    tile = part[j * VIEW_TOK : (j + 1) * VIEW_TOK]
                    at = base + j
                    total[at] = tile if total[at] is None else total[at] + tile
        for which, (total, kept) in enumerate(zip(sums, (own_k, own_v))):
            for j in range(local_views):
                rows = slice(j * VIEW_TOK, (j + 1) * VIEW_TOK)
                g_out[0, c, which, rows] = total[j].astype(jnp.bfloat16)
                g_out[1, c, which, rows] = total[2 * local_views + j].astype(jnp.bfloat16)
                kept[c, rows] = total[local_views + j]
        for side in (0, 1):
            grad_copy(c, side).start()
        return 0

    lax.fori_loop(0, chunks, work, 0)

    stores = [
        pltpu.make_async_copy(a_ref, a_hbm, stored.at[0]),
        pltpu.make_async_copy(gq_ref, gq_hbm, stored.at[1]),
    ]
    for copy in stores:
        copy.start()

    def part_store(c, which):
        src, dst = ((gk_ref, gk_hbm), (gv_ref, gv_hbm))[which]
        cols = columns(c)
        return pltpu.make_async_copy(
            src.at[:, cols], dst.at[:, cols], stored_part.at[which, c]
        )

    def finish(c, _):
        cols = columns(c)
        for side in (0, 1):
            grad_copy(c, side).wait_recv()
        for which, (kept, result) in enumerate(((own_k, gk_ref), (own_v, gv_ref))):
            total = (
                kept[c]
                + g_in[0, c, which].astype(jnp.float32)
                + g_in[1, c, which].astype(jnp.float32)
            )
            result[:, cols] = total.astype(jnp.bfloat16)
            part_store(c, which).start()
        return 0

    lax.fori_loop(0, chunks, finish, 0)

    def drain(c, _):
        for side in (0, 1):
            for which in (0, 1):
                kv_copy(c, side, which).wait_send()
            grad_copy(c, side).wait_send()
        for which in (0, 1):
            part_store(c, which).wait()
        return 0

    lax.fori_loop(0, chunks, drain, 0)
    for copy in stores:
        copy.wait()


def store(count, *refs):
    sources, targets, held = refs[:count], refs[count : 2 * count], refs[2 * count : 3 * count]
    loaded, stored = refs[3 * count :]
    loads = [pltpu.make_async_copy(sources[i], held[i], loaded.at[i]) for i in range(count)]
    stores = [pltpu.make_async_copy(held[i], targets[i], stored.at[i]) for i in range(count)]
    for load in loads:
        load.start()
    for i in range(count):
        loads[i].wait()
        stores[i].start()
    for copy in stores:
        copy.wait()


def body(queries, keys, values, grad_out, pairs, counts):
    size = lax.axis_size("view")
    span, width = queries.shape
    chunks = width // LANES
    assert span == REACH * VIEW_TOK
    hbm = pl.BlockSpec(memory_space=pltpu.HBM)

    def run(*refs):
        kernel(size, chunks, *refs)

    pair_flops = 2 * 6 * 2 * 2 * VIEW_TOK * 5 * VIEW_TOK * LANES
    block = jax.ShapeDtypeStruct((span, width), jnp.bfloat16)
    results = pl.pallas_call(
        run,
        name="windowed_attention",
        out_shape=[block] * 4,
        in_specs=[hbm] * 6,
        out_specs=[hbm] * 4,
        scratch_shapes=[
            pltpu.SMEM(pairs.shape, pairs.dtype),
            pltpu.SMEM(counts.shape, counts.dtype),
            pltpu.VMEM((span, width), jnp.bfloat16),
            pltpu.VMEM((span, width), jnp.bfloat16),
            pltpu.VMEM((span, width), jnp.bfloat16),
            pltpu.VMEM((span, width), jnp.bfloat16),
            pltpu.SemaphoreType.DMA((6,)),
            pltpu.VMEM((span, width), jnp.bfloat16),
            pltpu.VMEM((span, width), jnp.bfloat16),
            pltpu.VMEM((span, width), jnp.bfloat16),
            pltpu.VMEM((span, width), jnp.bfloat16),
            pltpu.SemaphoreType.DMA((2,)),
            pltpu.SemaphoreType.DMA((2, chunks)),
            pltpu.VMEM((2, chunks, span, LANES), jnp.bfloat16),
            pltpu.VMEM((2, chunks, span, LANES), jnp.bfloat16),
            pltpu.VMEM((2, chunks, 2, span, LANES), jnp.bfloat16),
            pltpu.VMEM((2, chunks, 2, span, LANES), jnp.bfloat16),
            pltpu.VMEM((chunks, span, LANES), jnp.float32),
            pltpu.VMEM((chunks, span, LANES), jnp.float32),
            pltpu.SemaphoreType.DMA((2, 2, chunks)),
            pltpu.SemaphoreType.DMA((2, 2, chunks)),
            pltpu.SemaphoreType.DMA((2, chunks)),
            pltpu.SemaphoreType.DMA((2, chunks)),
        ],
        cost_estimate=pl.CostEstimate(
            flops=chunks * pair_flops,
            bytes_accessed=8 * span * width * 2,
            transcendentals=chunks * 4 * VIEW_TOK * 5 * VIEW_TOK,
        ),
        compiler_params=pltpu.CompilerParams(
            collective_id=0, has_side_effects=True, vmem_limit_bytes=VMEM_BYTES
        ),
    )(pairs, counts, queries, keys, values, grad_out)
    return pl.pallas_call(
        functools.partial(store, 4),
        name="store_results",
        out_shape=[block] * 4,
        in_specs=[hbm] * 4,
        out_specs=[hbm] * 4,
        scratch_shapes=[pltpu.VMEM((span, width), jnp.bfloat16)] * 4
        + [pltpu.SemaphoreType.DMA((4,)), pltpu.SemaphoreType.DMA((4,))],
        compiler_params=pltpu.CompilerParams(vmem_limit_bytes=VMEM_BYTES),
    )(*results)


def solution(mesh):
    rows = P(("scene", "view"), None)
    return jax.shard_map(
        body,
        mesh=mesh,
        in_specs=(rows, rows, rows, rows, rows, P(("scene", "view"))),
        out_specs=(rows, rows, rows, rows),
        check_vma=False,
    )
```

```python
import functools

import jax
import jax.numpy as jnp
from jax import lax
from jax.experimental import pallas as pl
from jax.experimental.pallas import tpu as pltpu
from jax.sharding import PartitionSpec as P

HEAD_DIM = 64
VIEW_TOK = 128
LANES = 2 * HEAD_DIM
MASKED = -1e30
REACH = 2
VMEM_BYTES = 60 * 1024 * 1024


def nt(a, b):
    return lax.dot_general(a, b, (((1,), (1,)), ((), ())), preferred_element_type=jnp.float32)


def tn(a, b):
    return lax.dot_general(a, b, (((0,), (0,)), ((), ())), preferred_element_type=jnp.float32)


def nn(a, b):
    return jnp.dot(a, b, preferred_element_type=jnp.float32)


def two_heads(rows):
    first = lax.broadcasted_iota(jnp.int32, rows.shape, 1) < HEAD_DIM
    zero = jnp.zeros_like(rows)
    return jnp.concatenate([jnp.where(first, rows, zero), jnp.where(first, zero, rows)], axis=0)


def fold_heads(wide):
    first = lax.broadcasted_iota(jnp.int32, (LANES, VIEW_TOK), 0) < HEAD_DIM
    return jnp.where(first, wide[:, :VIEW_TOK], wide[:, VIEW_TOK:])


def block_bias(pairs, counts, view, own, views, offset):
    target = lax.rem(own + offset + views, views)
    live = jnp.bool_(False)
    for slot in range(pairs.shape[1]):
        live = live | ((pairs[view, slot] == target) & (slot < counts[view]))
    return jnp.where(live, 0.0, MASKED).astype(jnp.float32)


def attend(q, d, k_win, v_win, biases):
    qs = two_heads((q.astype(jnp.float32) * HEAD_DIM ** -0.5).astype(jnp.bfloat16))
    ds = two_heads(d)
    scores = nt(k_win, qs)
    tiles = []
    for j, bias in enumerate(biases):
        tile = scores[j * VIEW_TOK : (j + 1) * VIEW_TOK]
        tiles.append(tile if bias is None else tile + bias)
    scores = jnp.concatenate(tiles, axis=0)
    grown = jnp.exp(scores - jnp.max(scores, axis=0, keepdims=True))
    weights = grown * (1.0 / jnp.sum(grown, axis=0, keepdims=True))
    weights_b = weights.astype(jnp.bfloat16)
    out = fold_heads(tn(v_win, weights_b))
    product = out * d.astype(jnp.float32).T
    delta = jnp.concatenate(
        [
            jnp.sum(product[:HEAD_DIM], axis=0, keepdims=True),
            jnp.sum(product[HEAD_DIM:], axis=0, keepdims=True),
        ],
        axis=1,
    )
    score_grad = (weights * (nt(v_win, ds) - delta)).astype(jnp.bfloat16)
    grad_q = fold_heads(tn(k_win, score_grad)) * HEAD_DIM ** -0.5
    return (
        out.T.astype(jnp.bfloat16),
        grad_q.T.astype(jnp.bfloat16),
        nn(score_grad, qs),
        nn(weights_b, ds),
    )


def kernel(
    size, chunks,
    pairs_hbm, counts_hbm, q_hbm, k_hbm, v_hbm, d_hbm,
    a_hbm, gq_hbm, gk_hbm, gv_hbm,
    pairs, counts, q_ref, d_ref, kv_ref, fetched, kv_fetched,
    a_ref, gq_ref, gk_ref, gv_ref, stored, stored_part,
    kv_in, g_out, g_in, own_k, own_v,
    kv_send, kv_recv, g_send, g_recv,
):
    me = lax.axis_index("view")
    peers = (lax.rem(me + size - 1, size), lax.rem(me + 1, size))
    span = q_ref.shape[0]
    local_views = span // VIEW_TOK
    views = size * local_views

    def columns(c):
        return pl.ds(pl.multiple_of(c * LANES, LANES), LANES)

    def kv_fetch(c, which):
        return pltpu.make_async_copy(
            (k_hbm, v_hbm)[which].at[:, columns(c)], kv_ref.at[c, which], kv_fetched.at[which, c]
        )

    def fetch_all(c, _):
        for which in (0, 1):
            kv_fetch(c, which).start()
        return 0

    lax.fori_loop(0, chunks, fetch_all, 0)
    fetches = [
        pltpu.make_async_copy(src, dst, fetched.at[i])
        for i, (src, dst) in enumerate(
            (
                (q_hbm, q_ref),
                (d_hbm, d_ref),
                (pairs_hbm, pairs),
                (counts_hbm, counts),
            )
        )
    ]
    for fetch in fetches:
        fetch.start()

    barrier = pltpu.get_barrier_semaphore()
    for peer in peers:
        pl.semaphore_signal(
            barrier, inc=1, device_id={"view": peer}, device_id_type=pl.DeviceIdType.MESH
        )
    pl.semaphore_wait(barrier, 2)

    def kv_copy(c, side):
        return pltpu.make_async_remote_copy(
            src_ref=kv_ref.at[c],
            dst_ref=kv_in.at[1 - side, c],
            send_sem=kv_send.at[side, c],
            recv_sem=kv_recv.at[1 - side, c],
            device_id={"view": peers[side]},
            device_id_type=pl.DeviceIdType.MESH,
        )

    def grad_copy(c, side):
        return pltpu.make_async_remote_copy(
            src_ref=g_out.at[side, c],
            dst_ref=g_in.at[1 - side, c],
            send_sem=g_send.at[side, c],
            recv_sem=g_recv.at[1 - side, c],
            device_id={"view": peers[side]},
            device_id_type=pl.DeviceIdType.MESH,
        )

    def send_all(c, _):
        for which in (0, 1):
            kv_fetch(c, which).wait()
        for side in (0, 1):
            kv_copy(c, side).start()
        return 0

    lax.fori_loop(0, chunks, send_all, 0)

    for fetch in fetches:
        fetch.wait()
    biases = []
    for view in range(local_views):
        own = me * local_views + view
        biases.append(
            [
                None if offset == 0 else block_bias(pairs, counts, view, own, views, offset)
                for offset in range(-REACH, REACH + 1)
            ]
        )

    def work(c, _):
        for side in (0, 1):
            kv_copy(c, side).wait_recv()
        cols = columns(c)
        k_all, v_all = (
            jnp.concatenate([kv_in[0, c, which], kv_ref[c, which], kv_in[1, c, which]], axis=0)
            for which in (0, 1)
        )
        sums = [[None] * (3 * local_views), [None] * (3 * local_views)]
        for view in range(local_views):
            rows = slice(view * VIEW_TOK, (view + 1) * VIEW_TOK)
            base = local_views + view - REACH
            win = slice(base * VIEW_TOK, (base + 2 * REACH + 1) * VIEW_TOK)
            out, grad_q, part_k, part_v = attend(
                q_ref[rows, cols], d_ref[rows, cols], k_all[win], v_all[win], biases[view]
            )
            a_ref[rows, cols] = out
            gq_ref[rows, cols] = grad_q
            for total, part in zip(sums, (part_k, part_v)):
                for j in range(2 * REACH + 1):
                    tile = part[j * VIEW_TOK : (j + 1) * VIEW_TOK]
                    at = base + j
                    total[at] = tile if total[at] is None else total[at] + tile
        for which, (total, kept) in enumerate(zip(sums, (own_k, own_v))):
            for j in range(local_views):
                rows = slice(j * VIEW_TOK, (j + 1) * VIEW_TOK)
                g_out[0, c, which, rows] = total[j].astype(jnp.bfloat16)
                g_out[1, c, which, rows] = total[2 * local_views + j].astype(jnp.bfloat16)
                kept[c, rows] = total[local_views + j]
        for side in (0, 1):
            grad_copy(c, side).start()
        return 0

    lax.fori_loop(0, chunks, work, 0)

    stores = [
        pltpu.make_async_copy(a_ref, a_hbm, stored.at[0]),
        pltpu.make_async_copy(gq_ref, gq_hbm, stored.at[1]),
    ]
    for copy in stores:
        copy.start()

    def part_store(c, which):
        src, dst = ((gk_ref, gk_hbm), (gv_ref, gv_hbm))[which]
        cols = columns(c)
        return pltpu.make_async_copy(
            src.at[:, cols], dst.at[:, cols], stored_part.at[which, c]
        )

    def finish(c, _):
        cols = columns(c)
        for side in (0, 1):
            grad_copy(c, side).wait_recv()
        for which, (kept, result) in enumerate(((own_k, gk_ref), (own_v, gv_ref))):
            total = (
                kept[c]
                + g_in[0, c, which].astype(jnp.float32)
                + g_in[1, c, which].astype(jnp.float32)
            )
            result[:, cols] = total.astype(jnp.bfloat16)
            part_store(c, which).start()
        return 0

    lax.fori_loop(0, chunks, finish, 0)

    def drain(c, _):
        for side in (0, 1):
            kv_copy(c, side).wait_send()
            grad_copy(c, side).wait_send()
        for which in (0, 1):
            part_store(c, which).wait()
        return 0

    lax.fori_loop(0, chunks, drain, 0)
    for copy in stores:
        copy.wait()


def store(count, *refs):
    sources, targets, held = refs[:count], refs[count : 2 * count], refs[2 * count : 3 * count]
    loaded, stored = refs[3 * count :]
    loads = [pltpu.make_async_copy(sources[i], held[i], loaded.at[i]) for i in range(count)]
    stores = [pltpu.make_async_copy(held[i], targets[i], stored.at[i]) for i in range(count)]
    for load in loads:
        load.start()
    for i in range(count):
        loads[i].wait()
        stores[i].start()
    for copy in stores:
        copy.wait()


def body(queries, keys, values, grad_out, pairs, counts):
    size = lax.axis_size("view")
    span, width = queries.shape
    chunks = width // LANES
    assert span == REACH * VIEW_TOK
    hbm = pl.BlockSpec(memory_space=pltpu.HBM)

    def run(*refs):
        kernel(size, chunks, *refs)

    pair_flops = 2 * 6 * 2 * 2 * VIEW_TOK * 5 * VIEW_TOK * LANES
    block = jax.ShapeDtypeStruct((span, width), jnp.bfloat16)
    results = pl.pallas_call(
        run,
        name="windowed_attention",
        out_shape=[block] * 4,
        in_specs=[hbm] * 6,
        out_specs=[hbm] * 4,
        scratch_shapes=[
            pltpu.SMEM(pairs.shape, pairs.dtype),
            pltpu.SMEM(counts.shape, counts.dtype),
            pltpu.VMEM((span, width), jnp.bfloat16),
            pltpu.VMEM((span, width), jnp.bfloat16),
            pltpu.VMEM((chunks, 2, span, LANES), jnp.bfloat16),
            pltpu.SemaphoreType.DMA((4,)),
            pltpu.SemaphoreType.DMA((2, chunks)),
            pltpu.VMEM((span, width), jnp.bfloat16),
            pltpu.VMEM((span, width), jnp.bfloat16),
            pltpu.VMEM((span, width), jnp.bfloat16),
            pltpu.VMEM((span, width), jnp.bfloat16),
            pltpu.SemaphoreType.DMA((2,)),
            pltpu.SemaphoreType.DMA((2, chunks)),
            pltpu.VMEM((2, chunks, 2, span, LANES), jnp.bfloat16),
            pltpu.VMEM((2, chunks, 2, span, LANES), jnp.bfloat16),
            pltpu.VMEM((2, chunks, 2, span, LANES), jnp.bfloat16),
            pltpu.VMEM((chunks, span, LANES), jnp.float32),
            pltpu.VMEM((chunks, span, LANES), jnp.float32),
            pltpu.SemaphoreType.DMA((2, chunks)),
            pltpu.SemaphoreType.DMA((2, chunks)),
            pltpu.SemaphoreType.DMA((2, chunks)),
            pltpu.SemaphoreType.DMA((2, chunks)),
        ],
        cost_estimate=pl.CostEstimate(
            flops=chunks * pair_flops,
            bytes_accessed=8 * span * width * 2,
            transcendentals=chunks * 4 * VIEW_TOK * 5 * VIEW_TOK,
        ),
        compiler_params=pltpu.CompilerParams(
            collective_id=0, has_side_effects=True, vmem_limit_bytes=VMEM_BYTES
        ),
    )(pairs, counts, queries, keys, values, grad_out)
    return pl.pallas_call(
        functools.partial(store, 4),
        name="store_results",
        out_shape=[block] * 4,
        in_specs=[hbm] * 4,
        out_specs=[hbm] * 4,
        scratch_shapes=[pltpu.VMEM((span, width), jnp.bfloat16)] * 4
        + [pltpu.SemaphoreType.DMA((4,)), pltpu.SemaphoreType.DMA((4,))],
        compiler_params=pltpu.CompilerParams(vmem_limit_bytes=VMEM_BYTES),
    )(*results)


def solution(mesh):
    rows = P(("scene", "view"), None)
    return jax.shard_map(
        body,
        mesh=mesh,
        in_specs=(rows, rows, rows, rows, rows, P(("scene", "view"))),
        out_specs=(rows, rows, rows, rows),
        check_vma=False,
    )
```

```python
import functools

import jax
import jax.numpy as jnp
from jax import lax
from jax.experimental import pallas as pl
from jax.experimental.pallas import tpu as pltpu
from jax.sharding import PartitionSpec as P

HEAD_DIM = 64
VIEW_TOK = 128
LANES = 2 * HEAD_DIM
MASKED = -1e30
REACH = 2
VMEM_BYTES = 60 * 1024 * 1024


def nt(a, b):
    return lax.dot_general(a, b, (((1,), (1,)), ((), ())), preferred_element_type=jnp.float32)


def tn(a, b):
    return lax.dot_general(a, b, (((0,), (0,)), ((), ())), preferred_element_type=jnp.float32)


def nn(a, b):
    return jnp.dot(a, b, preferred_element_type=jnp.float32)


def two_heads(rows):
    first = lax.broadcasted_iota(jnp.int32, rows.shape, 1) < HEAD_DIM
    zero = jnp.zeros_like(rows)
    return jnp.concatenate([jnp.where(first, rows, zero), jnp.where(first, zero, rows)], axis=0)


def fold_heads(wide):
    first = lax.broadcasted_iota(jnp.int32, (LANES, VIEW_TOK), 0) < HEAD_DIM
    return jnp.where(first, wide[:, :VIEW_TOK], wide[:, VIEW_TOK:])


def block_bias(pairs, counts, view, own, views, offset):
    target = lax.rem(own + offset + views, views)
    live = jnp.bool_(False)
    for slot in range(pairs.shape[1]):
        live = live | ((pairs[view, slot] == target) & (slot < counts[view]))
    return jnp.where(live, 0.0, MASKED).astype(jnp.float32)


def attend(q, d, k_win, v_win, biases):
    qs = two_heads((q.astype(jnp.float32) * HEAD_DIM ** -0.5).astype(jnp.bfloat16))
    ds = two_heads(d)
    scores = nt(k_win, qs)
    tiles = []
    for j, bias in enumerate(biases):
        tile = scores[j * VIEW_TOK : (j + 1) * VIEW_TOK]
        tiles.append(tile if bias is None else tile + bias)
    scores = jnp.concatenate(tiles, axis=0)
    grown = jnp.exp(scores - jnp.max(scores, axis=0, keepdims=True))
    weights = grown * (1.0 / jnp.sum(grown, axis=0, keepdims=True))
    weights_b = weights.astype(jnp.bfloat16)
    out = fold_heads(tn(v_win, weights_b))
    product = out * d.astype(jnp.float32).T
    delta = jnp.concatenate(
        [
            jnp.sum(product[:HEAD_DIM], axis=0, keepdims=True),
            jnp.sum(product[HEAD_DIM:], axis=0, keepdims=True),
        ],
        axis=1,
    )
    score_grad = (weights * (nt(v_win, ds) - delta)).astype(jnp.bfloat16)
    grad_q = fold_heads(tn(k_win, score_grad)) * HEAD_DIM ** -0.5
    return (
        out.T.astype(jnp.bfloat16),
        grad_q.T.astype(jnp.bfloat16),
        nn(score_grad, qs),
        nn(weights_b, ds),
    )


def kernel(
    size, chunks,
    pairs_hbm, counts_hbm, q_hbm, k_hbm, v_hbm, d_hbm,
    a_hbm, gq_hbm, gk_hbm, gv_hbm,
    pairs, counts, q_ref, d_ref, kv_ref, fetched, kv_fetched,
    a_ref, gq_ref, gk_ref, gv_ref, stored, stored_part,
    kv_in, g_out, g_in, own_k, own_v,
    kv_send, kv_recv, g_send, g_recv,
):
    me = lax.axis_index("view")
    peers = (lax.rem(me + size - 1, size), lax.rem(me + 1, size))
    span = q_ref.shape[0]
    local_views = span // VIEW_TOK
    views = size * local_views

    def columns(c):
        return pl.ds(pl.multiple_of(c * LANES, LANES), LANES)

    def kv_fetch(c, which):
        return pltpu.make_async_copy(
            (k_hbm, v_hbm)[which].at[:, columns(c)], kv_ref.at[c, which], kv_fetched.at[which, c]
        )

    def fetch_all(c, _):
        for which in (0, 1):
            kv_fetch(c, which).start()
        return 0

    lax.fori_loop(0, chunks, fetch_all, 0)
    fetches = [
        pltpu.make_async_copy(src, dst, fetched.at[i])
        for i, (src, dst) in enumerate(
            (
                (q_hbm, q_ref),
                (d_hbm, d_ref),
                (pairs_hbm, pairs),
                (counts_hbm, counts),
            )
        )
    ]
    for fetch in fetches:
        fetch.start()

    barrier = pltpu.get_barrier_semaphore()
    for peer in peers:
        pl.semaphore_signal(
            barrier, inc=1, device_id={"view": peer}, device_id_type=pl.DeviceIdType.MESH
        )
    pl.semaphore_wait(barrier, 2)

    def kv_copy(c, side):
        return pltpu.make_async_remote_copy(
            src_ref=kv_ref.at[c],
            dst_ref=kv_in.at[1 - side, c],
            send_sem=kv_send.at[side, c],
            recv_sem=kv_recv.at[1 - side, c],
            device_id={"view": lax.rem(me + size - 1 + 2 * side, size)},
            device_id_type=pl.DeviceIdType.MESH,
        )

    def grad_copy(c, side):
        return pltpu.make_async_remote_copy(
            src_ref=g_out.at[side, c],
            dst_ref=g_in.at[1 - side, c],
            send_sem=g_send.at[side, c],
            recv_sem=g_recv.at[1 - side, c],
            device_id={"view": peers[side]},
            device_id_type=pl.DeviceIdType.MESH,
        )

    def send_all(c, _):
        for which in (0, 1):
            kv_fetch(c, which).wait()
        for turn in (0, 1):
            kv_copy(c, lax.rem(me + turn, 2)).start()
        return 0

    lax.fori_loop(0, chunks, send_all, 0)

    for fetch in fetches:
        fetch.wait()
    biases = []
    for view in range(local_views):
        own = me * local_views + view
        biases.append(
            [
                None if offset == 0 else block_bias(pairs, counts, view, own, views, offset)
                for offset in range(-REACH, REACH + 1)
            ]
        )

    def work(c, _):
        for side in (0, 1):
            kv_copy(c, side).wait_recv()
        cols = columns(c)
        k_all, v_all = (
            jnp.concatenate([kv_in[0, c, which], kv_ref[c, which], kv_in[1, c, which]], axis=0)
            for which in (0, 1)
        )
        sums = [[None] * (3 * local_views), [None] * (3 * local_views)]
        for view in range(local_views):
            rows = slice(view * VIEW_TOK, (view + 1) * VIEW_TOK)
            base = local_views + view - REACH
            win = slice(base * VIEW_TOK, (base + 2 * REACH + 1) * VIEW_TOK)
            out, grad_q, part_k, part_v = attend(
                q_ref[rows, cols], d_ref[rows, cols], k_all[win], v_all[win], biases[view]
            )
            a_ref[rows, cols] = out
            gq_ref[rows, cols] = grad_q
            for total, part in zip(sums, (part_k, part_v)):
                for j in range(2 * REACH + 1):
                    tile = part[j * VIEW_TOK : (j + 1) * VIEW_TOK]
                    at = base + j
                    total[at] = tile if total[at] is None else total[at] + tile
        for which, (total, kept) in enumerate(zip(sums, (own_k, own_v))):
            for j in range(local_views):
                rows = slice(j * VIEW_TOK, (j + 1) * VIEW_TOK)
                g_out[0, c, which, rows] = total[j].astype(jnp.bfloat16)
                g_out[1, c, which, rows] = total[2 * local_views + j].astype(jnp.bfloat16)
                kept[c, rows] = total[local_views + j]
        for side in (0, 1):
            grad_copy(c, side).start()
        return 0

    lax.fori_loop(0, chunks, work, 0)

    stores = [
        pltpu.make_async_copy(a_ref, a_hbm, stored.at[0]),
        pltpu.make_async_copy(gq_ref, gq_hbm, stored.at[1]),
    ]
    for copy in stores:
        copy.start()

    def part_store(c, which):
        src, dst = ((gk_ref, gk_hbm), (gv_ref, gv_hbm))[which]
        cols = columns(c)
        return pltpu.make_async_copy(
            src.at[:, cols], dst.at[:, cols], stored_part.at[which, c]
        )

    def finish(c, _):
        cols = columns(c)
        for side in (0, 1):
            grad_copy(c, side).wait_recv()
        for which, (kept, result) in enumerate(((own_k, gk_ref), (own_v, gv_ref))):
            total = (
                kept[c]
                + g_in[0, c, which].astype(jnp.float32)
                + g_in[1, c, which].astype(jnp.float32)
            )
            result[:, cols] = total.astype(jnp.bfloat16)
            part_store(c, which).start()
        return 0

    lax.fori_loop(0, chunks, finish, 0)

    def drain(c, _):
        for side in (0, 1):
            kv_copy(c, side).wait_send()
            grad_copy(c, side).wait_send()
        for which in (0, 1):
            part_store(c, which).wait()
        return 0

    lax.fori_loop(0, chunks, drain, 0)
    for copy in stores:
        copy.wait()


def store(count, *refs):
    sources, targets, held = refs[:count], refs[count : 2 * count], refs[2 * count : 3 * count]
    loaded, stored = refs[3 * count :]
    loads = [pltpu.make_async_copy(sources[i], held[i], loaded.at[i]) for i in range(count)]
    stores = [pltpu.make_async_copy(held[i], targets[i], stored.at[i]) for i in range(count)]
    for load in loads:
        load.start()
    for i in range(count):
        loads[i].wait()
        stores[i].start()
    for copy in stores:
        copy.wait()


def body(queries, keys, values, grad_out, pairs, counts):
    size = lax.axis_size("view")
    span, width = queries.shape
    chunks = width // LANES
    assert span == REACH * VIEW_TOK
    hbm = pl.BlockSpec(memory_space=pltpu.HBM)

    def run(*refs):
        kernel(size, chunks, *refs)

    pair_flops = 2 * 6 * 2 * 2 * VIEW_TOK * 5 * VIEW_TOK * LANES
    block = jax.ShapeDtypeStruct((span, width), jnp.bfloat16)
    results = pl.pallas_call(
        run,
        name="windowed_attention",
        out_shape=[block] * 4,
        in_specs=[hbm] * 6,
        out_specs=[hbm] * 4,
        scratch_shapes=[
            pltpu.SMEM(pairs.shape, pairs.dtype),
            pltpu.SMEM(counts.shape, counts.dtype),
            pltpu.VMEM((span, width), jnp.bfloat16),
            pltpu.VMEM((span, width), jnp.bfloat16),
            pltpu.VMEM((chunks, 2, span, LANES), jnp.bfloat16),
            pltpu.SemaphoreType.DMA((4,)),
            pltpu.SemaphoreType.DMA((2, chunks)),
            pltpu.VMEM((span, width), jnp.bfloat16),
            pltpu.VMEM((span, width), jnp.bfloat16),
            pltpu.VMEM((span, width), jnp.bfloat16),
            pltpu.VMEM((span, width), jnp.bfloat16),
            pltpu.SemaphoreType.DMA((2,)),
            pltpu.SemaphoreType.DMA((2, chunks)),
            pltpu.VMEM((2, chunks, 2, span, LANES), jnp.bfloat16),
            pltpu.VMEM((2, chunks, 2, span, LANES), jnp.bfloat16),
            pltpu.VMEM((2, chunks, 2, span, LANES), jnp.bfloat16),
            pltpu.VMEM((chunks, span, LANES), jnp.float32),
            pltpu.VMEM((chunks, span, LANES), jnp.float32),
            pltpu.SemaphoreType.DMA((2, chunks)),
            pltpu.SemaphoreType.DMA((2, chunks)),
            pltpu.SemaphoreType.DMA((2, chunks)),
            pltpu.SemaphoreType.DMA((2, chunks)),
        ],
        cost_estimate=pl.CostEstimate(
            flops=chunks * pair_flops,
            bytes_accessed=8 * span * width * 2,
            transcendentals=chunks * 4 * VIEW_TOK * 5 * VIEW_TOK,
        ),
        compiler_params=pltpu.CompilerParams(
            collective_id=0, has_side_effects=True, vmem_limit_bytes=VMEM_BYTES
        ),
    )(pairs, counts, queries, keys, values, grad_out)
    return pl.pallas_call(
        functools.partial(store, 4),
        name="store_results",
        out_shape=[block] * 4,
        in_specs=[hbm] * 4,
        out_specs=[hbm] * 4,
        scratch_shapes=[pltpu.VMEM((span, width), jnp.bfloat16)] * 4
        + [pltpu.SemaphoreType.DMA((4,)), pltpu.SemaphoreType.DMA((4,))],
        compiler_params=pltpu.CompilerParams(vmem_limit_bytes=VMEM_BYTES),
    )(*results)


def solution(mesh):
    rows = P(("scene", "view"), None)
    return jax.shard_map(
        body,
        mesh=mesh,
        in_specs=(rows, rows, rows, rows, rows, P(("scene", "view"))),
        out_specs=(rows, rows, rows, rows),
        check_vma=False,
    )
```

```python
import functools

import jax
import jax.numpy as jnp
from jax import lax
from jax.experimental import pallas as pl
from jax.experimental.pallas import tpu as pltpu
from jax.sharding import PartitionSpec as P

HEAD_DIM = 64
VIEW_TOK = 128
LANES = 2 * HEAD_DIM
MASKED = -1e30
REACH = 2
VMEM_BYTES = 60 * 1024 * 1024


def nt(a, b):
    return lax.dot_general(a, b, (((1,), (1,)), ((), ())), preferred_element_type=jnp.float32)


def tn(a, b):
    return lax.dot_general(a, b, (((0,), (0,)), ((), ())), preferred_element_type=jnp.float32)


def nn(a, b):
    return jnp.dot(a, b, preferred_element_type=jnp.float32)


def two_heads(rows):
    first = lax.broadcasted_iota(jnp.int32, rows.shape, 1) < HEAD_DIM
    zero = jnp.zeros_like(rows)
    return jnp.concatenate([jnp.where(first, rows, zero), jnp.where(first, zero, rows)], axis=0)


def fold_heads(wide):
    first = lax.broadcasted_iota(jnp.int32, (LANES, VIEW_TOK), 0) < HEAD_DIM
    return jnp.where(first, wide[:, :VIEW_TOK], wide[:, VIEW_TOK:])


def block_bias(pairs, counts, view, own, views, offset):
    target = lax.rem(own + offset + views, views)
    live = jnp.bool_(False)
    for slot in range(pairs.shape[1]):
        live = live | ((pairs[view, slot] == target) & (slot < counts[view]))
    return jnp.where(live, 0.0, MASKED).astype(jnp.float32)


def attend(q, d, k_win, v_win, biases):
    qs = two_heads((q.astype(jnp.float32) * HEAD_DIM ** -0.5).astype(jnp.bfloat16))
    ds = two_heads(d)
    scores = nt(k_win, qs)
    tiles = []
    for j, bias in enumerate(biases):
        tile = scores[j * VIEW_TOK : (j + 1) * VIEW_TOK]
        tiles.append(tile if bias is None else tile + bias)
    scores = jnp.concatenate(tiles, axis=0)
    grown = jnp.exp(scores - jnp.max(scores, axis=0, keepdims=True))
    weights = grown * (1.0 / jnp.sum(grown, axis=0, keepdims=True))
    weights_b = weights.astype(jnp.bfloat16)
    out = fold_heads(tn(v_win, weights_b))
    product = out * d.astype(jnp.float32).T
    delta = jnp.concatenate(
        [
            jnp.sum(product[:HEAD_DIM], axis=0, keepdims=True),
            jnp.sum(product[HEAD_DIM:], axis=0, keepdims=True),
        ],
        axis=1,
    )
    score_grad = (weights * (nt(v_win, ds) - delta)).astype(jnp.bfloat16)
    grad_q = fold_heads(tn(k_win, score_grad)) * HEAD_DIM ** -0.5
    return (
        out.T.astype(jnp.bfloat16),
        grad_q.T.astype(jnp.bfloat16),
        nn(score_grad, qs),
        nn(weights_b, ds),
    )


def kernel(
    size, chunks,
    pairs_hbm, counts_hbm, q_hbm, k_hbm, v_hbm, d_hbm,
    a_hbm, gq_hbm, gk_hbm, gv_hbm,
    pairs, counts, q_ref, d_ref, kv_ref, fetched, kv_fetched,
    a_ref, gq_ref, gk_ref, gv_ref, stored, stored_part,
    kv_in, g_out, g_in, own_k, own_v,
    kv_send, kv_recv, g_send, g_recv,
):
    me = lax.axis_index("view")
    peers = (lax.rem(me + size - 1, size), lax.rem(me + 1, size))
    span = q_ref.shape[0]
    local_views = span // VIEW_TOK
    views = size * local_views

    def columns(c):
        return pl.ds(pl.multiple_of(c * LANES, LANES), LANES)

    def kv_fetch(c, which):
        return pltpu.make_async_copy(
            (k_hbm, v_hbm)[which].at[:, columns(c)], kv_ref.at[c, which], kv_fetched.at[which, c]
        )

    def fetch_all(c, _):
        for which in (0, 1):
            kv_fetch(c, which).start()
        return 0

    lax.fori_loop(0, chunks, fetch_all, 0)
    fetches = [
        pltpu.make_async_copy(src, dst, fetched.at[i])
        for i, (src, dst) in enumerate(
            (
                (q_hbm, q_ref),
                (d_hbm, d_ref),
                (pairs_hbm, pairs),
                (counts_hbm, counts),
            )
        )
    ]
    for fetch in fetches:
        fetch.start()

    barrier = pltpu.get_barrier_semaphore()
    for peer in peers:
        pl.semaphore_signal(
            barrier, inc=1, device_id={"view": peer}, device_id_type=pl.DeviceIdType.MESH
        )
    pl.semaphore_wait(barrier, 2)

    def kv_copy(c, side):
        return pltpu.make_async_remote_copy(
            src_ref=kv_ref.at[c],
            dst_ref=kv_in.at[1 - side, c],
            send_sem=kv_send.at[side, c],
            recv_sem=kv_recv.at[1 - side, c],
            device_id={"view": lax.rem(me + size - 1 + 2 * side, size)},
            device_id_type=pl.DeviceIdType.MESH,
        )

    def grad_copy(c, side):
        return pltpu.make_async_remote_copy(
            src_ref=g_out.at[side, c],
            dst_ref=g_in.at[1 - side, c],
            send_sem=g_send.at[side, c],
            recv_sem=g_recv.at[1 - side, c],
            device_id={"view": peers[side]},
            device_id_type=pl.DeviceIdType.MESH,
        )

    def send_all(c, _):
        for which in (0, 1):
            kv_fetch(c, which).wait()
        for turn in (0, 1):
            kv_copy(c, lax.rem(me + turn, 2)).start()
        return 0

    lax.fori_loop(0, chunks, send_all, 0)

    for fetch in fetches:
        fetch.wait()
    biases = []
    for view in range(local_views):
        own = me * local_views + view
        biases.append(
            [
                None if offset == 0 else block_bias(pairs, counts, view, own, views, offset)
                for offset in range(-REACH, REACH + 1)
            ]
        )

    def work(c, _):
        for side in (0, 1):
            kv_copy(c, side).wait_recv()
        cols = columns(c)
        k_all, v_all = (
            jnp.concatenate([kv_in[0, c, which], kv_ref[c, which], kv_in[1, c, which]], axis=0)
            for which in (0, 1)
        )
        sums = [[None] * (3 * local_views), [None] * (3 * local_views)]
        for view in range(local_views):
            rows = slice(view * VIEW_TOK, (view + 1) * VIEW_TOK)
            base = local_views + view - REACH
            win = slice(base * VIEW_TOK, (base + 2 * REACH + 1) * VIEW_TOK)
            out, grad_q, part_k, part_v = attend(
                q_ref[rows, cols], d_ref[rows, cols], k_all[win], v_all[win], biases[view]
            )
            a_ref[rows, cols] = out
            gq_ref[rows, cols] = grad_q
            for total, part in zip(sums, (part_k, part_v)):
                for j in range(2 * REACH + 1):
                    tile = part[j * VIEW_TOK : (j + 1) * VIEW_TOK]
                    at = base + j
                    total[at] = tile if total[at] is None else total[at] + tile
        for which, (total, kept) in enumerate(zip(sums, (own_k, own_v))):
            for j in range(local_views):
                rows = slice(j * VIEW_TOK, (j + 1) * VIEW_TOK)
                g_out[0, c, which, rows] = total[j].astype(jnp.bfloat16)
                g_out[1, c, which, rows] = total[2 * local_views + j].astype(jnp.bfloat16)
                kept[c, rows] = total[local_views + j]
        for side in (0, 1):
            grad_copy(c, side).start()
        return 0

    lax.fori_loop(0, chunks, work, 0)

    stores = [
        pltpu.make_async_copy(a_ref, a_hbm, stored.at[0]),
        pltpu.make_async_copy(gq_ref, gq_hbm, stored.at[1]),
    ]
    for copy in stores:
        copy.start()

    def part_store(c, which):
        src, dst = ((gk_ref, gk_hbm), (gv_ref, gv_hbm))[which]
        cols = columns(c)
        return pltpu.make_async_copy(
            src.at[:, cols], dst.at[:, cols], stored_part.at[which, c]
        )

    def finish(c, _):
        cols = columns(c)
        for side in (0, 1):
            grad_copy(c, side).wait_recv()
        for which, (kept, result) in enumerate(((own_k, gk_ref), (own_v, gv_ref))):
            total = (
                kept[c]
                + g_in[0, c, which].astype(jnp.float32)
                + g_in[1, c, which].astype(jnp.float32)
            )
            result[:, cols] = total.astype(jnp.bfloat16)
            part_store(c, which).start()
        return 0

    lax.fori_loop(0, chunks, finish, 0)

    def drain(c, _):
        for side in (0, 1):
            kv_copy(c, side).wait_send()
            grad_copy(c, side).wait_send()
        for which in (0, 1):
            part_store(c, which).wait()
        return 0

    lax.fori_loop(0, chunks, drain, 0)
    for copy in stores:
        copy.wait()


def store(count, *refs):
    sources, targets, held = refs[:count], refs[count : 2 * count], refs[2 * count : 3 * count]
    loaded, stored = refs[3 * count :]
    half = held[0].shape[0] // 2
    pieces = [(i, pl.ds(part * half, half)) for i in range(count) for part in (0, 1)]
    loads = [
        pltpu.make_async_copy(sources[i].at[rows], held[i].at[rows], loaded.at[n])
        for n, (i, rows) in enumerate(pieces)
    ]
    stores = [
        pltpu.make_async_copy(held[i].at[rows], targets[i].at[rows], stored.at[n])
        for n, (i, rows) in enumerate(pieces)
    ]
    for load in loads:
        load.start()
    for load, copy in zip(loads, stores):
        load.wait()
        copy.start()
    for copy in stores:
        copy.wait()


def body(queries, keys, values, grad_out, pairs, counts):
    size = lax.axis_size("view")
    span, width = queries.shape
    chunks = width // LANES
    assert span == REACH * VIEW_TOK
    hbm = pl.BlockSpec(memory_space=pltpu.HBM)

    def run(*refs):
        kernel(size, chunks, *refs)

    pair_flops = 2 * 6 * 2 * 2 * VIEW_TOK * 5 * VIEW_TOK * LANES
    block = jax.ShapeDtypeStruct((span, width), jnp.bfloat16)
    results = pl.pallas_call(
        run,
        name="windowed_attention",
        out_shape=[block] * 4,
        in_specs=[hbm] * 6,
        out_specs=[hbm] * 4,
        scratch_shapes=[
            pltpu.SMEM(pairs.shape, pairs.dtype),
            pltpu.SMEM(counts.shape, counts.dtype),
            pltpu.VMEM((span, width), jnp.bfloat16),
            pltpu.VMEM((span, width), jnp.bfloat16),
            pltpu.VMEM((chunks, 2, span, LANES), jnp.bfloat16),
            pltpu.SemaphoreType.DMA((4,)),
            pltpu.SemaphoreType.DMA((2, chunks)),
            pltpu.VMEM((span, width), jnp.bfloat16),
            pltpu.VMEM((span, width), jnp.bfloat16),
            pltpu.VMEM((span, width), jnp.bfloat16),
            pltpu.VMEM((span, width), jnp.bfloat16),
            pltpu.SemaphoreType.DMA((2,)),
            pltpu.SemaphoreType.DMA((2, chunks)),
            pltpu.VMEM((2, chunks, 2, span, LANES), jnp.bfloat16),
            pltpu.VMEM((2, chunks, 2, span, LANES), jnp.bfloat16),
            pltpu.VMEM((2, chunks, 2, span, LANES), jnp.bfloat16),
            pltpu.VMEM((chunks, span, LANES), jnp.float32),
            pltpu.VMEM((chunks, span, LANES), jnp.float32),
            pltpu.SemaphoreType.DMA((2, chunks)),
            pltpu.SemaphoreType.DMA((2, chunks)),
            pltpu.SemaphoreType.DMA((2, chunks)),
            pltpu.SemaphoreType.DMA((2, chunks)),
        ],
        cost_estimate=pl.CostEstimate(
            flops=chunks * pair_flops,
            bytes_accessed=8 * span * width * 2,
            transcendentals=chunks * 4 * VIEW_TOK * 5 * VIEW_TOK,
        ),
        compiler_params=pltpu.CompilerParams(
            collective_id=0, has_side_effects=True, vmem_limit_bytes=VMEM_BYTES
        ),
    )(pairs, counts, queries, keys, values, grad_out)
    return pl.pallas_call(
        functools.partial(store, 4),
        name="store_results",
        out_shape=[block] * 4,
        in_specs=[hbm] * 4,
        out_specs=[hbm] * 4,
        scratch_shapes=[pltpu.VMEM((span, width), jnp.bfloat16)] * 4
        + [pltpu.SemaphoreType.DMA((8,)), pltpu.SemaphoreType.DMA((8,))],
        compiler_params=pltpu.CompilerParams(vmem_limit_bytes=VMEM_BYTES),
    )(*results)


def solution(mesh):
    rows = P(("scene", "view"), None)
    return jax.shard_map(
        body,
        mesh=mesh,
        in_specs=(rows, rows, rows, rows, rows, P(("scene", "view"))),
        out_specs=(rows, rows, rows, rows),
        check_vma=False,
    )
```
